32 devices in a mesh: ia: 4 (over z), ja: 4 (over y, core), ka: 2 (over x).
Axes of the slice: x: 2, y: 2, z: 4, core: 2. Of those that a mesh axis runs over, the one named last changes fastest.
Arguments:
- features: bfloat16 [768, 6144], P('ia', ('ka', 'ja')), may hold values from -6 to 6
- in_weight: bfloat16 [6144, 24576], P(('ka', 'ia'), 'ja'), may hold values from -0.078125 to 0.078125
- out_weight: bfloat16 [24576, 6144], P(('ja', 'ia'), 'ka'), may hold values from -0.0390625 to 0.0390625
- cotangent: bfloat16 [768, 6144], P('ia', ('ka', 'ja')), may hold values from -1.5 to 1.5
Outputs:
- layer_out: bfloat16 [768, 6144], P('ia', ('ka', 'ja'))
- feature_grad: bfloat16 [768, 6144], P('ia', ('ka', 'ja'))
- in_weight_grad: bfloat16 [6144, 24576], P(('ka', 'ia'), 'ja')
- out_weight_grad: bfloat16 [24576, 6144], P(('ja', 'ia'), 'ka')
The draws below stay inside these ranges and needn't reach their ends.
All inputs are finite; a program needn't handle non-finite values.
Results may differ from the reference program's by a relative error of at most 0.028.
Values may be sent and summed in bfloat16 or wider, within the bound.
No kernel may reach another device: no remote copies, remote signals or barrier semaphores. Data moves between devices by JAX's collectives and lax.ppermute only.
A program may use at most 192 MiB of HBM per device.

```python
import jax
import jax.numpy as jnp
from jax import lax

D = 6144
FF = 24576
ROWS = 192
TOKENS = 768
N_IA = 4


def steps_of(own_key, dims, cuts, least, largest):
    factor_of, own = 1.0, jax.random.fold_in(own_key, 6)
    for position, blocks in cuts:
        draws = jnp.exp(jax.random.uniform(jax.random.fold_in(own, position), (blocks,), jnp.float32, least / len(cuts), largest / len(cuts)))
        factor_of = factor_of * jnp.repeat(draws, dims[position] // blocks).reshape([-1 if axis == position else 1 for axis in range(len(dims))])
    return factor_of


def noise(rng, shape, width, bound, pieces=(), held_as=jnp.bfloat16):
    result = width * jax.random.normal(rng, shape, jnp.float32)
    if pieces:
        result = result * steps_of(rng, shape, pieces, -0.22, 0.18)
    return jnp.clip(result, -bound, bound).astype(held_as)


def setup_inputs(seed: int = 0) -> dict:
    streams_of = jax.random.split(jax.random.key(seed), 5)
    return {
        "features": noise(streams_of[0], (TOKENS, D), 1.0, 6.0, ((0, 4), (1, 8))),
        "in_weight": noise(streams_of[1], (D, FF), D ** -0.5, 0.078125, ((0, 8), (1, 4))),
        "out_weight": noise(streams_of[2], (FF, D), FF ** -0.5, 0.0390625, ((0, 16), (1, 2))),
        "cotangent": noise(streams_of[3], (TOKENS, D), 0.25, 1.5, ((0, 4), (1, 8))),
    }


GELU_SCALE = 0.7978845608028654


def gelu_value(hidden):
    inner = GELU_SCALE * (hidden + 0.044715 * hidden * hidden * hidden)
    return 0.5 * hidden * (1.0 + jnp.tanh(inner))


def gelu_slope(hidden):
    tangent = jnp.tanh(GELU_SCALE * (hidden + 0.044715 * hidden * hidden * hidden))
    return 0.5 * (1.0 + tangent) + 0.5 * hidden * (1.0 - tangent * tangent) * GELU_SCALE * (1.0 + 3.0 * 0.044715 * hidden * hidden)


def transposed(left, right):
    return lax.dot_general(left, right, (((1,), (1,)), ((), ())), preferred_element_type=jnp.float32)


def inner_rows(left, right):
    return lax.dot_general(left, right, (((0,), (0,)), ((), ())), preferred_element_type=jnp.float32)


def reference(features, in_weight, out_weight, cotangent):
    pre = jnp.dot(features, in_weight, preferred_element_type=jnp.float32)
    active = gelu_value(pre).astype(jnp.bfloat16)
    layer_out = jnp.dot(active, out_weight, preferred_element_type=jnp.float32).astype(jnp.bfloat16)
    grad_active = transposed(cotangent, out_weight)
    grad_pre = (grad_active * gelu_slope(pre)).astype(jnp.bfloat16)
    feature_grad = transposed(grad_pre, in_weight).astype(jnp.bfloat16)
    in_sum = jnp.zeros(in_weight.shape, jnp.float32)
    out_sum = jnp.zeros(out_weight.shape, jnp.float32)
    for group in range(N_IA):
        low = group * ROWS
        term_in = inner_rows(features[low:low + ROWS], grad_pre[low:low + ROWS]).astype(jnp.bfloat16)
        in_sum = in_sum + lax.optimization_barrier(term_in).astype(jnp.float32)
        term_out = inner_rows(active[low:low + ROWS], cotangent[low:low + ROWS]).astype(jnp.bfloat16)
        out_sum = out_sum + lax.optimization_barrier(term_out).astype(jnp.float32)
    return layer_out, feature_grad, in_sum.astype(jnp.bfloat16), out_sum.astype(jnp.bfloat16)
```

```python
import functools

import jax
import jax.numpy as jnp
from jax import lax
from jax.experimental import pallas as pl
from jax.experimental.pallas import tpu as pltpu
from jax.sharding import PartitionSpec as P

GELU_SCALE = 0.7978845608028654
VMEM_BYTES = 48 * 1024 * 1024


def gelu_value(hidden):
    inner = GELU_SCALE * (hidden + 0.044715 * hidden * hidden * hidden)
    return 0.5 * hidden * (1.0 + jnp.tanh(inner))


def gelu_slope(hidden):
    tangent = jnp.tanh(GELU_SCALE * (hidden + 0.044715 * hidden * hidden * hidden))
    return 0.5 * (1.0 + tangent) + 0.5 * hidden * (1.0 - tangent * tangent) * GELU_SCALE * (
        1.0 + 3.0 * 0.044715 * hidden * hidden
    )


def transposed(left, right):
    return lax.dot_general(
        left, right, (((1,), (1,)), ((), ())), preferred_element_type=jnp.float32
    )


def inner_rows(left, right):
    return lax.dot_general(
        left, right, (((0,), (0,)), ((), ())), preferred_element_type=jnp.float32
    )


def flip(block, axis, size, bit):
    return lax.ppermute(block, axis, [(d, d ^ bit) for d in range(size)])


def reversed_bits(size):
    order = [0]
    bit = size // 2
    while bit:
        order = [o for o in order] + [o + bit for o in order]
        bit //= 2
    return order


def column_tile(width):
    for tile in (768, 512, 384, 256, 128):
        if width % tile == 0:
            return tile
    return width


def nothing(block, *refs):
    del block, refs


def after(block, *earlier):
    return pl.pallas_call(
        nothing,
        out_shape=jax.ShapeDtypeStruct(block.shape, block.dtype),
        in_specs=[pl.BlockSpec(memory_space=pl.ANY)] * (1 + len(earlier)),
        out_specs=pl.BlockSpec(memory_space=pl.ANY),
        input_output_aliases={0: 0},
        cost_estimate=pl.CostEstimate(flops=0, bytes_accessed=0, transcendentals=0),
    )(block, *earlier)


def up_kernel(order, rows, weight, keep, send):
    del order
    part = jnp.dot(rows[...], weight[...], preferred_element_type=jnp.float32)
    half = part.shape[0] // 2
    keep[...] = part[:half].reshape(keep.shape)
    send[...] = part[half:].reshape(send.shape).astype(send.dtype)


def up_parts(order, rows, weight, halves, count, blocks):
    depth, width = weight.shape
    span = width // blocks
    tile = column_tile(span)
    tiles = span // tile
    shape = (halves, blocks, count, span)
    place = pl.BlockSpec((halves, None, count, tile), lambda b, n, order: (0, b, 0, n))
    return pl.pallas_call(
        up_kernel,
        grid_spec=pltpu.PrefetchScalarGridSpec(
            num_scalar_prefetch=1,
            grid=(blocks, tiles),
            in_specs=[
                pl.BlockSpec(rows.shape, lambda b, n, order: (0, 0)),
                pl.BlockSpec((depth, tile), lambda b, n, order: (0, order[b] * tiles + n)),
            ],
            out_specs=[place, place],
        ),
        out_shape=[
            jax.ShapeDtypeStruct(shape, jnp.float32),
            jax.ShapeDtypeStruct(shape, jnp.bfloat16),
        ],
        compiler_params=pltpu.CompilerParams(vmem_limit_bytes=VMEM_BYTES),
        cost_estimate=pl.CostEstimate(
            flops=2 * rows.shape[0] * depth * width,
            bytes_accessed=2 * depth * width + 6 * halves * count * width,
            transcendentals=0,
        ),
    )(order, rows, weight)


def block_kernel(order, rows, weight, out):
    del order
    part = jnp.dot(rows[...], weight[...], preferred_element_type=jnp.float32)
    out[...] = part.astype(out.dtype)


def up_blocks(order, rows, weight, blocks, kind):
    depth, width = weight.shape
    span = width // blocks
    tile = column_tile(span)
    tiles = span // tile
    chosen, count = order.shape[0], rows.shape[0]
    return pl.pallas_call(
        block_kernel,
        grid_spec=pltpu.PrefetchScalarGridSpec(
            num_scalar_prefetch=1,
            grid=(chosen, tiles),
            in_specs=[
                pl.BlockSpec(rows.shape, lambda b, n, order: (0, 0)),
                pl.BlockSpec((depth, tile), lambda b, n, order: (0, order[b] * tiles + n)),
            ],
            out_specs=pl.BlockSpec((None, count, tile), lambda b, n, order: (b, 0, n)),
        ),
        out_shape=jax.ShapeDtypeStruct((chosen, count, span), kind),
        compiler_params=pltpu.CompilerParams(vmem_limit_bytes=VMEM_BYTES),
        cost_estimate=pl.CostEstimate(
            flops=2 * count * depth * span * chosen,
            bytes_accessed=2 * chosen * span * (depth + 2 * count),
            transcendentals=0,
        ),
    )(order, rows, weight)


def down_kernel(order, rows, weight, keep, send, total):
    del order
    step = pl.program_id(1)
    part = transposed(rows[...], weight[...])

    @pl.when(step == 0)
    def _():
        total[...] = part

    @pl.when(step > 0)
    def _():
        total[...] += part

    @pl.when(step == pl.num_programs(1) - 1)
    def _():
        half = total.shape[0] // 2
        keep[...] = total[:half].reshape(keep.shape)
        send[...] = total[half:].reshape(send.shape).astype(send.dtype)


def down_parts(order, rows, weight, parts):
    blocks, tokens, span = rows.shape
    width = weight.shape[0]
    tile = next(t for t in (512, 384, 256, 128) if width % t == 0)
    shape = (parts // 2, tokens // parts, width)
    place = pl.BlockSpec(shape[:2] + (tile,), lambda n, b, order: (0, 0, n))
    return pl.pallas_call(
        down_kernel,
        grid_spec=pltpu.PrefetchScalarGridSpec(
            num_scalar_prefetch=1,
            grid=(width // tile, blocks),
            in_specs=[
                pl.BlockSpec((None, tokens, span), lambda n, b, order: (b, 0, 0)),
                pl.BlockSpec((tile, span), lambda n, b, order: (n, order[b])),
            ],
            out_specs=[place, place],
            scratch_shapes=[pltpu.VMEM((tokens, tile), jnp.float32)],
        ),
        out_shape=[
            jax.ShapeDtypeStruct(shape, jnp.float32),
            jax.ShapeDtypeStruct(shape, jnp.bfloat16),
        ],
        compiler_params=pltpu.CompilerParams(vmem_limit_bytes=VMEM_BYTES),
        cost_estimate=pl.CostEstimate(
            flops=2 * tokens * width * blocks * span,
            bytes_accessed=2 * blocks * span * (width + 3 * tokens) + 3 * tokens * width,
            transcendentals=0,
        ),
    )(order, rows, weight)


def active_kernel(keep, got, active):
    pre = keep[...] + got[...].astype(jnp.float32)
    active[...] = gelu_value(pre).astype(active.dtype)


def slope_kernel(keep, got, grad_keep, grad_got, grad):
    pre = keep[...] + got[...].astype(jnp.float32)
    above = grad_keep[...] + grad_got[...].astype(jnp.float32)
    grad[...] = (above * gelu_slope(pre)).astype(grad.dtype)


def on_chunk(kernel, arrays, place):
    count, span = arrays[0].shape
    tile = column_tile(span)
    here = pl.BlockSpec((count, tile), lambda n: (0, n))
    there = pl.BlockSpec((count, tile), lambda n: (place, n))
    return pl.pallas_call(
        kernel,
        grid=(span // tile,),
        in_specs=[here, here] + [there] * (len(arrays) - 2),
        out_specs=here,
        out_shape=jax.ShapeDtypeStruct((count, span), jnp.bfloat16),
        compiler_params=pltpu.CompilerParams(vmem_limit_bytes=VMEM_BYTES),
        cost_estimate=pl.CostEstimate(
            flops=20 * count * span,
            bytes_accessed=8 * count * span,
            transcendentals=count * span,
        ),
    )(*arrays)


def input_kernel(order, weight, *refs):
    del order
    pieces, out, total, stack = refs[:-3], refs[-3], refs[-2], refs[-1]
    first = (pl.program_id(0) == 0) & (pl.program_id(1) == 0)
    last = (pl.program_id(0) == pl.num_programs(0) - 1) & (
        pl.program_id(1) == pl.num_programs(1) - 1
    )

    @pl.when(first)
    def _():
        total[...] = jnp.zeros_like(total)

    row = 0
    for piece in pieces:
        for part in range(piece.shape[0]):
            stack[pl.ds(row, piece.shape[1]), :] = piece[part]
            row += piece.shape[1]
    total[...] += transposed(stack[...], weight[...])

    @pl.when(last)
    def _():
        out[...] = total[...].astype(out.dtype)


def input_parts(order, pieces, weight, blocks):
    depth, width = weight.shape
    span = width // blocks
    tile = column_tile(span)
    tiles = span // tile
    rows = sum(piece.shape[0] * piece.shape[2] for piece in pieces)
    return pl.pallas_call(
        input_kernel,
        grid_spec=pltpu.PrefetchScalarGridSpec(
            num_scalar_prefetch=1,
            grid=(blocks, tiles),
            in_specs=[
                pl.BlockSpec((depth, tile), lambda b, n, order: (0, order[b] * tiles + n))
            ]
            + [
                pl.BlockSpec(
                    (piece.shape[0], None, piece.shape[2], tile), lambda b, n, order: (0, b, 0, n)
                )
                for piece in pieces
            ],
            out_specs=pl.BlockSpec((rows, depth), lambda b, n, order: (0, 0)),
            scratch_shapes=[
                pltpu.VMEM((rows, depth), jnp.float32),
                pltpu.VMEM((rows, tile), jnp.bfloat16),
            ],
        ),
        out_shape=jax.ShapeDtypeStruct((rows, depth), jnp.bfloat16),
        compiler_params=pltpu.CompilerParams(vmem_limit_bytes=VMEM_BYTES),
        cost_estimate=pl.CostEstimate(
            flops=2 * rows * depth * width,
            bytes_accessed=2 * depth * width + 2 * rows * (depth + width),
            transcendentals=0,
        ),
    )(order, weight, *pieces)


def weight_kernel(order, columns, *refs):
    del order
    pieces, out, stack = refs[:-2], refs[-2], refs[-1]
    row = 0
    for piece in pieces:
        for part in range(piece.shape[0]):
            stack[pl.ds(row, piece.shape[1]), :] = piece[part]
            row += piece.shape[1]
    out[...] = jnp.dot(
        columns[...], stack[...], preferred_element_type=jnp.float32
    ).astype(out.dtype)


def weight_parts(order, columns, pieces, blocks):
    depth, rows = columns.shape
    span = pieces[0].shape[3]
    tile = column_tile(span)
    tiles = span // tile
    width = span * blocks
    return pl.pallas_call(
        weight_kernel,
        grid_spec=pltpu.PrefetchScalarGridSpec(
            num_scalar_prefetch=1,
            grid=(blocks, tiles),
            in_specs=[pl.BlockSpec((depth, rows), lambda b, n, order: (0, 0))]
            + [
                pl.BlockSpec(
                    (piece.shape[0], None, piece.shape[2], tile), lambda b, n, order: (0, b, 0, n)
                )
                for piece in pieces
            ],
            out_specs=pl.BlockSpec(
                (depth, tile), lambda b, n, order: (0, order[b] * tiles + n)
            ),
            scratch_shapes=[pltpu.VMEM((rows, tile), jnp.bfloat16)],
        ),
        out_shape=jax.ShapeDtypeStruct((depth, width), jnp.bfloat16),
        compiler_params=pltpu.CompilerParams(vmem_limit_bytes=VMEM_BYTES),
        cost_estimate=pl.CostEstimate(
            flops=2 * rows * depth * width,
            bytes_accessed=2 * rows * (depth + width) + 2 * depth * width,
            transcendentals=0,
        ),
    )(order, columns, *pieces)


def relative(parts, own):
    return jnp.stack(
        [
            lax.dynamic_index_in_dim(parts, own ^ s, 0, keepdims=False)
            for s in range(parts.shape[0])
        ]
    )


def halved(keep, send, axis, size, bit, down):
    while True:
        got = flip(send, axis, size, bit)
        if keep.shape[0] == 1:
            return keep[0], got[0]
        total = keep + got.astype(jnp.float32)
        half = total.shape[0] // 2
        keep, send = total[:half], total[half:].astype(jnp.bfloat16)
        bit = bit // 2 if down else bit * 2


def doubled(block, axis, size, up=False):
    bits = [1 << b for b in range(size.bit_length() - 1)]
    for bit in bits if up else bits[::-1]:
        block = jnp.concatenate([block, flip(block, axis, size, bit)], axis=0)
    return block


def natural(parts):
    return jnp.stack([parts[s] for s in reversed_bits(parts.shape[0])])


def local(ni, nj, nk, features, in_weight, out_weight, cotangent):
    tokens = features.shape[0] * ni
    depth = in_weight.shape[0]
    share = tokens // nk
    chunks = next(c for c in (4, 2, 1) if share % (16 * c) == 0)
    count = share // chunks
    own_i = lax.axis_index("ia")
    own_j = lax.axis_index("ja")
    own_k = lax.axis_index("ka")
    order = own_i ^ jnp.array(reversed_bits(ni), jnp.int32)
    swap = [(a * nj + b, b * ni + a) for a in range(ni) for b in range(nj)]
    crosswise = [chunk == 1 for chunk in range(chunks)]

    if ni == nj:
        turned = lax.ppermute(features, ("ia", "ja"), swap)
        feature_cols = lax.all_gather(turned, "ja", axis=0, tiled=True)
    else:
        feature_rows = lax.all_gather(features, "ja", axis=1, tiled=True)
        feature_cols = lax.all_to_all(
            feature_rows, "ia", split_axis=1, concat_axis=0, tiled=True
        )
    shuffled = relative(feature_cols.reshape(nk, share, depth), own_k)
    shuffled = shuffled.reshape(nk, chunks, count, depth).transpose(1, 0, 2, 3)
    shuffled = shuffled.reshape(tokens, depth)

    half = ni // 2
    straight = [chunk for chunk in range(chunks) if not crosswise[chunk]]
    across = [chunk for chunk in range(chunks) if crosswise[chunk]]
    rows_of = [shuffled[c * nk * count : (c + 1) * nk * count] for c in range(chunks)]
    kept = {}
    for chunk in straight:
        rows = rows_of[chunk]
        if chunk != straight[0]:
            rows = after(rows, kept[straight[0]][1])
        kept[chunk] = up_parts(order, rows, in_weight, nk // 2, count, ni)
    totals = {}
    for chunk in across:
        rows = after(rows_of[chunk], kept[straight[0]][1])
        send = up_blocks(order[half:], rows, in_weight, ni, jnp.bfloat16)
        keep = up_blocks(order[:half], rows, in_weight, ni, jnp.float32)
        keep, got = halved(keep, send, "ia", ni, 1, False)
        totals[chunk] = (keep + got.astype(jnp.float32)).reshape(nk, count, -1)

    if ni == nj:
        cotangent = after(cotangent, turned)
    cot_tokens = relative(natural(doubled(cotangent[None], "ia", ni)), own_i)
    cot_tokens = relative(cot_tokens.reshape(nk, share, -1), own_k)
    cot_tokens = after(cot_tokens.reshape(1, tokens, -1), kept[straight[0]][1])
    cot_parts = doubled(cot_tokens, "ja", nj)
    cot_order = own_j ^ jnp.array(reversed_bits(nj), jnp.int32)
    if cot_parts.shape[-1] % 128:
        cot_parts = relative(natural(cot_parts), own_j).transpose(1, 0, 2)
        cot_parts = cot_parts.reshape(1, tokens, -1)
        cot_order = jnp.zeros((1,), jnp.int32)
    grad_keep, grad_send = down_parts(cot_order, cot_parts, out_weight, nk)

    sums = [None] * chunks
    came = None
    for chunk in straight + across:
        if crosswise[chunk]:
            total = totals[chunk]
            send = after(total[nk // 2 :].astype(jnp.bfloat16), came)
            sums[chunk] = halved(total[: nk // 2], send, "ka", nk, nk // 2, True)
            came = sums[chunk][1]
        else:
            keep, send = kept[chunk]
            send = send if came is None else after(send, came)
            keep, came = halved(keep, send, "ka", nk, nk // 2, True)
            total = keep + came.astype(jnp.float32)
            sums[chunk] = halved(
                total[:half], total[half:].astype(jnp.bfloat16), "ia", ni, 1, False
            )
    grad_keep, grad_got = halved(
        grad_keep, after(grad_send, came), "ka", nk, nk // 2, True
    )
    actives = [on_chunk(active_kernel, sums[chunk], 0) for chunk in range(chunks)]
    parts = after(jnp.concatenate(actives, axis=0), grad_got)[None]
    active_rows = doubled(parts, "ka", nk, True).reshape(tokens, -1)
    came = active_rows

    firsts = {}
    for chunk in straight + across:
        arrays = list(sums[chunk]) + [grad_keep, grad_got]
        block = on_chunk(slope_kernel, arrays, chunk)[None]
        if crosswise[chunk]:
            block = doubled(block, "ka", nk, True).reshape(1, nk * count, -1)
        bit = ni // 2
        firsts[chunk] = jnp.concatenate([block, flip(block, "ia", ni, bit)], axis=0)
    turned_blocks = {}
    for chunk in straight + across:
        block = firsts[chunk]
        bit = ni // 4
        while bit:
            block = jnp.concatenate([block, flip(block, "ia", ni, bit)], axis=0)
            bit //= 2
        turned_blocks[chunk] = block

    columns = active_rows.T
    out_weight_grad = weight_parts(
        cot_order, columns, [cot_parts[None]], cot_parts.shape[0]
    )
    pieces_of = {}
    input_rows = [None] * chunks
    for place, chunk in enumerate(straight):
        earlier = [came]
        if place + 1 < len(straight):
            earlier.append(firsts[straight[place + 1]])
        if place == 0:
            gate = earlier[-1]
        if place == 2:
            earlier += [input_rows[straight[0]], out_weight_grad]
        block = after(turned_blocks[chunk][None], *earlier)
        pieces = [block]
        bit = 1
        while bit < nk:
            came = flip(block, "ka", nk, bit)
            pieces.append(came)
            bit *= 2
            if bit < nk:
                block = jnp.concatenate([block, came], axis=0)
        pieces_of[chunk] = pieces
        if place == len(straight) - 1:
            for other in across:
                block = turned_blocks[other]
                pieces_of[other] = [block.reshape(1, ni, nk * count, -1)]
                input_rows[other] = input_parts(order, pieces_of[other], in_weight, ni)
            done = [rows for rows in input_rows if rows is not None]
            if done:
                pieces = [after(pieces[0], *done)] + pieces[1:]
        input_rows[chunk] = input_parts(order, pieces, in_weight, ni)
    input_rows = [rows.reshape(nk, count, depth) for rows in input_rows]
    in_weight_grad = weight_parts(
        order,
        shuffled.T,
        [piece for chunk in range(chunks) for piece in pieces_of[chunk]],
        ni,
    )

    input_part = jnp.stack(input_rows, axis=1).reshape(nk, share, depth)
    input_part = relative(input_part, own_k).reshape(tokens, depth)
    if ni == nj:
        parts = natural(relative(input_part.reshape(nj, tokens // nj, depth), own_j))
        keep, got = halved(parts[: nj // 2], parts[nj // 2 :], "ja", nj, 1, False)
        input_sum = (keep + got.astype(jnp.float32)).astype(jnp.bfloat16)
        feature_grad = lax.ppermute(input_sum, ("ia", "ja"), swap)
    else:
        input_full = lax.all_to_all(
            input_part, "ia", split_axis=0, concat_axis=1, tiled=True
        )
        feature_grad = lax.psum_scatter(
            input_full, "ja", scatter_dimension=1, tiled=True
        )

    active_rows = after(active_rows, gate)
    output_part = jnp.dot(active_rows, out_weight, preferred_element_type=jnp.float32)
    output_cols = lax.psum_scatter(
        output_part.astype(jnp.bfloat16), "ja", scatter_dimension=1, tiled=True
    )
    output_cols = relative(output_cols.reshape(nk, share, -1), own_k)
    layer_out = lax.psum_scatter(
        output_cols.reshape(tokens, -1), "ia", scatter_dimension=0, tiled=True
    )
    return (layer_out, feature_grad, in_weight_grad, out_weight_grad)


def solution(mesh):
    placed = (
        P("ia", ("ka", "ja")),
        P(("ka", "ia"), "ja"),
        P(("ja", "ia"), "ka"),
        P("ia", ("ka", "ja")),
    )
    return jax.shard_map(
        functools.partial(local, *(mesh.shape[axis] for axis in ("ia", "ja", "ka"))),
        mesh=mesh,
        in_specs=placed,
        out_specs=(
            P("ia", ("ka", "ja")),
            P("ia", ("ka", "ja")),
            P(("ka", "ia"), "ja"),
            P(("ja", "ia"), "ka"),
        ),
        check_vma=False,
    )
```

```python
import functools

import jax
import jax.numpy as jnp
from jax import lax
from jax.experimental import pallas as pl
from jax.experimental.pallas import tpu as pltpu
from jax.sharding import PartitionSpec as P

GELU_SCALE = 0.7978845608028654
VMEM_BYTES = 48 * 1024 * 1024


def gelu_value(hidden):
    inner = GELU_SCALE * (hidden + 0.044715 * hidden * hidden * hidden)
    return 0.5 * hidden * (1.0 + jnp.tanh(inner))


def gelu_slope(hidden):
    tangent = jnp.tanh(GELU_SCALE * (hidden + 0.044715 * hidden * hidden * hidden))
    return 0.5 * (1.0 + tangent) + 0.5 * hidden * (1.0 - tangent * tangent) * GELU_SCALE * (
        1.0 + 3.0 * 0.044715 * hidden * hidden
    )


def transposed(left, right):
    return lax.dot_general(
        left, right, (((1,), (1,)), ((), ())), preferred_element_type=jnp.float32
    )


def inner_rows(left, right):
    return lax.dot_general(
        left, right, (((0,), (0,)), ((), ())), preferred_element_type=jnp.float32
    )


def flip(block, axis, size, bit):
    return lax.ppermute(block, axis, [(d, d ^ bit) for d in range(size)])


def reversed_bits(size):
    order = [0]
    bit = size // 2
    while bit:
        order = [o for o in order] + [o + bit for o in order]
        bit //= 2
    return order


def column_tile(width):
    for tile in (768, 512, 384, 256, 128):
        if width % tile == 0:
            return tile
    return width


def nothing(block, *refs):
    del block, refs


def after(block, *earlier):
    return pl.pallas_call(
        nothing,
        out_shape=jax.ShapeDtypeStruct(block.shape, block.dtype),
        in_specs=[pl.BlockSpec(memory_space=pl.ANY)] * (1 + len(earlier)),
        out_specs=pl.BlockSpec(memory_space=pl.ANY),
        input_output_aliases={0: 0},
        cost_estimate=pl.CostEstimate(flops=0, bytes_accessed=0, transcendentals=0),
    )(block, *earlier)


def up_kernel(order, rows, weight, keep, send):
    del order
    part = jnp.dot(rows[...], weight[...], preferred_element_type=jnp.float32)
    half = part.shape[0] // 2
    keep[...] = part[:half].reshape(keep.shape)
    send[...] = part[half:].reshape(send.shape).astype(send.dtype)


def up_parts(order, rows, weight, halves, count, blocks):
    depth, width = weight.shape
    span = width // blocks
    tile = column_tile(span)
    tiles = span // tile
    shape = (halves, blocks, count, span)
    place = pl.BlockSpec((halves, None, count, tile), lambda b, n, order: (0, b, 0, n))
    return pl.pallas_call(
        up_kernel,
        grid_spec=pltpu.PrefetchScalarGridSpec(
            num_scalar_prefetch=1,
            grid=(blocks, tiles),
            in_specs=[
                pl.BlockSpec(rows.shape, lambda b, n, order: (0, 0)),
                pl.BlockSpec((depth, tile), lambda b, n, order: (0, order[b] * tiles + n)),
            ],
            out_specs=[place, place],
        ),
        out_shape=[
            jax.ShapeDtypeStruct(shape, jnp.float32),
            jax.ShapeDtypeStruct(shape, jnp.bfloat16),
        ],
        compiler_params=pltpu.CompilerParams(vmem_limit_bytes=VMEM_BYTES),
        cost_estimate=pl.CostEstimate(
            flops=2 * rows.shape[0] * depth * width,
            bytes_accessed=2 * depth * width + 6 * halves * count * width,
            transcendentals=0,
        ),
    )(order, rows, weight)


def block_kernel(order, rows, weight, out):
    del order
    part = jnp.dot(rows[...], weight[...], preferred_element_type=jnp.float32)
    out[...] = part.astype(out.dtype)


def up_blocks(order, rows, weight, blocks, kind):
    depth, width = weight.shape
    span = width // blocks
    tile = column_tile(span)
    tiles = span // tile
    chosen, count = order.shape[0], rows.shape[0]
    return pl.pallas_call(
        block_kernel,
        grid_spec=pltpu.PrefetchScalarGridSpec(
            num_scalar_prefetch=1,
            grid=(chosen, tiles),
            in_specs=[
                pl.BlockSpec(rows.shape, lambda b, n, order: (0, 0)),
                pl.BlockSpec((depth, tile), lambda b, n, order: (0, order[b] * tiles + n)),
            ],
            out_specs=pl.BlockSpec((None, count, tile), lambda b, n, order: (b, 0, n)),
        ),
        out_shape=jax.ShapeDtypeStruct((chosen, count, span), kind),
        compiler_params=pltpu.CompilerParams(vmem_limit_bytes=VMEM_BYTES),
        cost_estimate=pl.CostEstimate(
            flops=2 * count * depth * span * chosen,
            bytes_accessed=2 * chosen * span * (depth + 2 * count),
            transcendentals=0,
        ),
    )(order, rows, weight)


def down_kernel(order, rows, weight, keep, send, total):
    del order
    step = pl.program_id(1)
    part = transposed(rows[...], weight[...])

    @pl.when(step == 0)
    def _():
        total[...] = part

    @pl.when(step > 0)
    def _():
        total[...] += part

    @pl.when(step == pl.num_programs(1) - 1)
    def _():
        half = total.shape[0] // 2
        keep[...] = total[:half].reshape(keep.shape)
        send[...] = total[half:].reshape(send.shape).astype(send.dtype)


def down_parts(order, rows, weight, parts):
    blocks, tokens, span = rows.shape
    width = weight.shape[0]
    tile = next(t for t in (512, 384, 256, 128) if width % t == 0)
    shape = (parts // 2, tokens // parts, width)
    place = pl.BlockSpec(shape[:2] + (tile,), lambda n, b, order: (0, 0, n))
    return pl.pallas_call(
        down_kernel,
        grid_spec=pltpu.PrefetchScalarGridSpec(
            num_scalar_prefetch=1,
            grid=(width // tile, blocks),
            in_specs=[
                pl.BlockSpec((None, tokens, span), lambda n, b, order: (b, 0, 0)),
                pl.BlockSpec((tile, span), lambda n, b, order: (n, order[b])),
            ],
            out_specs=[place, place],
            scratch_shapes=[pltpu.VMEM((tokens, tile), jnp.float32)],
        ),
        out_shape=[
            jax.ShapeDtypeStruct(shape, jnp.float32),
            jax.ShapeDtypeStruct(shape, jnp.bfloat16),
        ],
        compiler_params=pltpu.CompilerParams(vmem_limit_bytes=VMEM_BYTES),
        cost_estimate=pl.CostEstimate(
            flops=2 * tokens * width * blocks * span,
            bytes_accessed=2 * blocks * span * (width + 3 * tokens) + 3 * tokens * width,
            transcendentals=0,
        ),
    )(order, rows, weight)


def active_kernel(keep, got, active):
    pre = keep[...] + got[...].astype(jnp.float32)
    active[...] = gelu_value(pre).astype(active.dtype)


def slope_kernel(keep, got, grad_keep, grad_got, grad):
    pre = keep[...] + got[...].astype(jnp.float32)
    above = grad_keep[...] + grad_got[...].astype(jnp.float32)
    grad[...] = (above * gelu_slope(pre)).astype(grad.dtype)


def on_chunk(kernel, arrays, place):
    count, span = arrays[0].shape
    tile = column_tile(span)
    here = pl.BlockSpec((count, tile), lambda n: (0, n))
    there = pl.BlockSpec((count, tile), lambda n: (place, n))
    return pl.pallas_call(
        kernel,
        grid=(span // tile,),
        in_specs=[here, here] + [there] * (len(arrays) - 2),
        out_specs=here,
        out_shape=jax.ShapeDtypeStruct((count, span), jnp.bfloat16),
        compiler_params=pltpu.CompilerParams(vmem_limit_bytes=VMEM_BYTES),
        cost_estimate=pl.CostEstimate(
            flops=20 * count * span,
            bytes_accessed=8 * count * span,
            transcendentals=count * span,
        ),
    )(*arrays)


def input_kernel(order, weight, *refs):
    del order
    pieces, out, total, stack = refs[:-3], refs[-3], refs[-2], refs[-1]
    first = (pl.program_id(0) == 0) & (pl.program_id(1) == 0)
    last = (pl.program_id(0) == pl.num_programs(0) - 1) & (
        pl.program_id(1) == pl.num_programs(1) - 1
    )

    @pl.when(first)
    def _():
        total[...] = jnp.zeros_like(total)

    row = 0
    for piece in pieces:
        for part in range(piece.shape[0]):
            stack[pl.ds(row, piece.shape[1]), :] = piece[part]
            row += piece.shape[1]
    total[...] += transposed(stack[...], weight[...])

    @pl.when(last)
    def _():
        out[...] = total[...].astype(out.dtype)


def input_parts(order, pieces, weight, blocks):
    depth, width = weight.shape
    span = width // blocks
    tile = column_tile(span)
    tiles = span // tile
    rows = sum(piece.shape[0] * piece.shape[2] for piece in pieces)
    return pl.pallas_call(
        input_kernel,
        grid_spec=pltpu.PrefetchScalarGridSpec(
            num_scalar_prefetch=1,
            grid=(blocks, tiles),
            in_specs=[
                pl.BlockSpec((depth, tile), lambda b, n, order: (0, order[b] * tiles + n))
            ]
            + [
                pl.BlockSpec(
                    (piece.shape[0], None, piece.shape[2], tile), lambda b, n, order: (0, b, 0, n)
                )
                for piece in pieces
            ],
            out_specs=pl.BlockSpec((rows, depth), lambda b, n, order: (0, 0)),
            scratch_shapes=[
                pltpu.VMEM((rows, depth), jnp.float32),
                pltpu.VMEM((rows, tile), jnp.bfloat16),
            ],
        ),
        out_shape=jax.ShapeDtypeStruct((rows, depth), jnp.bfloat16),
        compiler_params=pltpu.CompilerParams(vmem_limit_bytes=VMEM_BYTES),
        cost_estimate=pl.CostEstimate(
            flops=2 * rows * depth * width,
            bytes_accessed=2 * depth * width + 2 * rows * (depth + width),
            transcendentals=0,
        ),
    )(order, weight, *pieces)


def weight_kernel(order, columns, *refs):
    del order
    pieces, out, stack = refs[:-2], refs[-2], refs[-1]
    row = 0
    for piece in pieces:
        for part in range(piece.shape[0]):
            stack[pl.ds(row, piece.shape[1]), :] = piece[part]
            row += piece.shape[1]
    out[...] = jnp.dot(
        columns[...], stack[...], preferred_element_type=jnp.float32
    ).astype(out.dtype)


def weight_parts(order, columns, pieces, blocks):
    depth, rows = columns.shape
    span = pieces[0].shape[3]
    tile = column_tile(span)
    tiles = span // tile
    width = span * blocks
    return pl.pallas_call(
        weight_kernel,
        grid_spec=pltpu.PrefetchScalarGridSpec(
            num_scalar_prefetch=1,
            grid=(blocks, tiles),
            in_specs=[pl.BlockSpec((depth, rows), lambda b, n, order: (0, 0))]
            + [
                pl.BlockSpec(
                    (piece.shape[0], None, piece.shape[2], tile), lambda b, n, order: (0, b, 0, n)
                )
                for piece in pieces
            ],
            out_specs=pl.BlockSpec(
                (depth, tile), lambda b, n, order: (0, order[b] * tiles + n)
            ),
            scratch_shapes=[pltpu.VMEM((rows, tile), jnp.bfloat16)],
        ),
        out_shape=jax.ShapeDtypeStruct((depth, width), jnp.bfloat16),
        compiler_params=pltpu.CompilerParams(vmem_limit_bytes=VMEM_BYTES),
        cost_estimate=pl.CostEstimate(
            flops=2 * rows * depth * width,
            bytes_accessed=2 * rows * (depth + width) + 2 * depth * width,
            transcendentals=0,
        ),
    )(order, columns, *pieces)


def relative(parts, own):
    return jnp.stack(
        [
            lax.dynamic_index_in_dim(parts, own ^ s, 0, keepdims=False)
            for s in range(parts.shape[0])
        ]
    )


def halved(keep, send, axis, size, bit, down):
    while True:
        got = flip(send, axis, size, bit)
        if keep.shape[0] == 1:
            return keep[0], got[0]
        total = keep + got.astype(jnp.float32)
        half = total.shape[0] // 2
        keep, send = total[:half], total[half:].astype(jnp.bfloat16)
        bit = bit // 2 if down else bit * 2


def doubled(block, axis, size, up=False):
    bits = [1 << b for b in range(size.bit_length() - 1)]
    for bit in bits if up else bits[::-1]:
        block = jnp.concatenate([block, flip(block, axis, size, bit)], axis=0)
    return block


def natural(parts):
    return jnp.stack([parts[s] for s in reversed_bits(parts.shape[0])])


def local(ni, nj, nk, features, in_weight, out_weight, cotangent):
    tokens = features.shape[0] * ni
    depth = in_weight.shape[0]
    share = tokens // nk
    chunks = next(c for c in (4, 2, 1) if share % (16 * c) == 0)
    count = share // chunks
    own_i = lax.axis_index("ia")
    own_j = lax.axis_index("ja")
    own_k = lax.axis_index("ka")
    order = own_i ^ jnp.array(reversed_bits(ni), jnp.int32)
    swap = [(a * nj + b, b * ni + a) for a in range(ni) for b in range(nj)]
    crosswise = [chunk == 1 for chunk in range(chunks)]

    if ni == nj:
        turned = lax.ppermute(features, ("ia", "ja"), swap)
        feature_cols = lax.all_gather(turned, "ja", axis=0, tiled=True)
    else:
        feature_rows = lax.all_gather(features, "ja", axis=1, tiled=True)
        feature_cols = lax.all_to_all(
            feature_rows, "ia", split_axis=1, concat_axis=0, tiled=True
        )
    shuffled = relative(feature_cols.reshape(nk, share, depth), own_k)
    shuffled = shuffled.reshape(nk, chunks, count, depth).transpose(1, 0, 2, 3)
    shuffled = shuffled.reshape(tokens, depth)

    half = ni // 2
    straight = [chunk for chunk in range(chunks) if not crosswise[chunk]]
    across = [chunk for chunk in range(chunks) if crosswise[chunk]]
    rows_of = [shuffled[c * nk * count : (c + 1) * nk * count] for c in range(chunks)]
    kept = {}
    arrived = []

    def product(place):
        rows = rows_of[straight[place]]
        if place == 1:
            rows = after(rows, kept[straight[0]][1])
        if place > 1:
            rows = after(rows, arrived[place - 2])
        kept[straight[place]] = up_parts(order, rows, in_weight, nk // 2, count, ni)

    product(0)
    if len(straight) > 1:
        product(1)
    begun = kept[straight[:2][-1]][1]
    crossing = {}
    for chunk in across:
        rows = after(rows_of[chunk], begun)
        send = up_blocks(order[half:], rows, in_weight, ni, jnp.bfloat16)
        keep = up_blocks(order[:half], rows, in_weight, ni, jnp.float32)
        crossing[chunk] = halved(keep, send, "ia", ni, 1, False)

    if ni == nj:
        cotangent = after(cotangent, turned)
    cot_tokens = relative(natural(doubled(cotangent[None], "ia", ni)), own_i)
    cot_tokens = relative(cot_tokens.reshape(nk, share, -1), own_k)
    cot_tokens = after(cot_tokens.reshape(1, tokens, -1), begun)
    cot_parts = doubled(cot_tokens, "ja", nj)
    cot_order = own_j ^ jnp.array(reversed_bits(nj), jnp.int32)
    if cot_parts.shape[-1] % 128:
        cot_parts = relative(natural(cot_parts), own_j).transpose(1, 0, 2)
        cot_parts = cot_parts.reshape(1, tokens, -1)
        cot_order = jnp.zeros((1,), jnp.int32)
    grad_keep, grad_send = down_parts(cot_order, cot_parts, out_weight, nk)

    sums = [None] * chunks
    for place, chunk in enumerate(straight):
        if place > 1:
            product(place)
        keep, send = kept[chunk]
        if place:
            send = after(send, arrived[-1])
        keep, came = halved(keep, send, "ka", nk, nk // 2, True)
        arrived.append(came)
        total = keep + came.astype(jnp.float32)
        sums[chunk] = halved(
            total[:half], total[half:].astype(jnp.bfloat16), "ia", ni, 1, False
        )
    came = arrived[-1]
    for chunk, later in zip(straight, arrived[1:]):
        keep, got = sums[chunk]
        sums[chunk] = keep, after(got, later)
    for chunk in across:
        keep, got = crossing[chunk]
        got = after(got, arrived[-2:][0])
        total = (keep + got.astype(jnp.float32)).reshape(nk, count, -1)
        send = after(total[nk // 2 :].astype(jnp.bfloat16), came, grad_send)
        sums[chunk] = halved(total[: nk // 2], send, "ka", nk, nk // 2, True)
        came = sums[chunk][1]
    grad_keep, grad_got = halved(
        grad_keep, after(grad_send, came), "ka", nk, nk // 2, True
    )
    actives = [on_chunk(active_kernel, sums[chunk], 0) for chunk in range(chunks)]
    parts = after(jnp.concatenate(actives, axis=0), grad_got)[None]
    active_parts = doubled(parts, "ka", nk, True)
    active_rows = active_parts.reshape(tokens, -1)
    came = active_parts

    slopes = {}
    slope = None
    for chunk in range(chunks):
        arrays = list(sums[chunk]) + [grad_keep, grad_got]
        if slope is not None:
            arrays[1] = after(arrays[1], slope)
        slope = on_chunk(slope_kernel, arrays, chunk)
        slopes[chunk] = slope[None]
    gathered = [
        lax.all_gather(slopes[chunk], "ia", axis=0, tiled=True) for chunk in range(chunks)
    ]
    plain = jnp.arange(ni, dtype=jnp.int32)

    def output_over_ja(*gates):
        active_tokens = relative(active_parts, own_k).reshape(ni, tokens // ni, -1)
        active_tokens = natural(relative(active_tokens, own_i)).reshape(tokens, -1)
        active_tokens = after(active_tokens, *gates)
        if out_weight.shape[1] // nj % 128:
            output_part = jnp.dot(
                active_tokens, out_weight, preferred_element_type=jnp.float32
            )
            output_sum = lax.psum_scatter(
                output_part.astype(jnp.bfloat16), "ja", scatter_dimension=1, tiled=True
            ).astype(jnp.float32)
        else:
            send = up_blocks(
                cot_order[nj // 2 :], active_tokens, out_weight, nj, jnp.bfloat16
            )
            keep = up_blocks(
                cot_order[: nj // 2], active_tokens, out_weight, nj, jnp.float32
            )
            keep, got = halved(keep, send, "ja", nj, 1, False)
            output_sum = keep + got.astype(jnp.float32)
        return output_sum

    pieces_of = []
    input_rows = []
    for chunk in range(chunks):
        ready = slopes[chunks - 1] if chunk == 0 else came
        block = after(gathered[chunk][None], came, ready, *input_rows[-2:-1])
        pieces = [block]
        bit = 1
        while bit < nk:
            came = flip(block, "ka", nk, bit)
            pieces.append(came)
            bit *= 2
            if bit < nk:
                block = jnp.concatenate([block, came], axis=0)
        arrived.append(came)
        pieces_of.append(pieces)
        if chunk == 0:
            output_sum = output_over_ja(came, gathered[: chunks // 2][-1])
        if chunk == chunks - 1:
            pieces = [after(pieces[0], output_sum, *input_rows)] + pieces[1:]
        input_rows.append(input_parts(plain, pieces, in_weight, ni))
    last_rows = input_rows[-1]
    late = arrived[-2:][0]
    out_weight_grad = weight_parts(
        cot_order, after(active_rows.T, late), [cot_parts[None]], cot_parts.shape[0]
    )
    input_rows = [rows.reshape(nk, count, depth) for rows in input_rows]
    in_weight_grad = weight_parts(
        plain,
        after(shuffled.T, last_rows),
        [piece for pieces in pieces_of for piece in pieces],
        ni,
    )

    input_part = jnp.stack(input_rows, axis=1).reshape(nk, share, depth)
    input_part = relative(input_part, own_k).reshape(tokens, depth)
    if ni == nj:
        parts = natural(relative(input_part.reshape(nj, tokens // nj, depth), own_j))
        keep, got = halved(parts[: nj // 2], parts[nj // 2 :], "ja", nj, 1, False)
        input_sum = (keep + got.astype(jnp.float32)).astype(jnp.bfloat16)
        feature_grad = lax.ppermute(input_sum, ("ia", "ja"), swap)
    else:
        input_full = lax.all_to_all(
            input_part, "ia", split_axis=0, concat_axis=1, tiled=True
        )
        feature_grad = lax.psum_scatter(
            input_full, "ja", scatter_dimension=1, tiled=True
        )

    output_sum = output_sum.reshape(ni, tokens // ni, -1)
    send = output_sum[half:].astype(jnp.bfloat16)
    keep, got = halved(output_sum[:half], send, "ia", ni, 1, False)
    layer_out = (keep + got.astype(jnp.float32)).astype(jnp.bfloat16)
    return (layer_out, feature_grad, in_weight_grad, out_weight_grad)


def solution(mesh):
    placed = (
        P("ia", ("ka", "ja")),
        P(("ka", "ia"), "ja"),
        P(("ja", "ia"), "ka"),
        P("ia", ("ka", "ja")),
    )
    return jax.shard_map(
        functools.partial(local, *(mesh.shape[axis] for axis in ("ia", "ja", "ka"))),
        mesh=mesh,
        in_specs=placed,
        out_specs=(
            P("ia", ("ka", "ja")),
            P("ia", ("ka", "ja")),
            P(("ka", "ia"), "ja"),
            P(("ja", "ia"), "ka"),
        ),
        check_vma=False,
    )
```

```python
import functools

import jax
import jax.numpy as jnp
from jax import lax
from jax.experimental import pallas as pl
from jax.experimental.pallas import tpu as pltpu
from jax.sharding import PartitionSpec as P

GELU_SCALE = 0.7978845608028654
VMEM_BYTES = 48 * 1024 * 1024


def gelu_value(hidden):
    inner = GELU_SCALE * (hidden + 0.044715 * hidden * hidden * hidden)
    return 0.5 * hidden * (1.0 + jnp.tanh(inner))


def gelu_slope(hidden):
    tangent = jnp.tanh(GELU_SCALE * (hidden + 0.044715 * hidden * hidden * hidden))
    return 0.5 * (1.0 + tangent) + 0.5 * hidden * (1.0 - tangent * tangent) * GELU_SCALE * (
        1.0 + 3.0 * 0.044715 * hidden * hidden
    )


def transposed(left, right):
    return lax.dot_general(
        left, right, (((1,), (1,)), ((), ())), preferred_element_type=jnp.float32
    )


def inner_rows(left, right):
    return lax.dot_general(
        left, right, (((0,), (0,)), ((), ())), preferred_element_type=jnp.float32
    )


def flip(block, axis, size, bit):
    return lax.ppermute(block, axis, [(d, d ^ bit) for d in range(size)])


def reversed_bits(size):
    order = [0]
    bit = size // 2
    while bit:
        order = [o for o in order] + [o + bit for o in order]
        bit //= 2
    return order


def column_tile(width):
    for tile in (768, 512, 384, 256, 128):
        if width % tile == 0:
            return tile
    return width


def nothing(block, *refs):
    del block, refs


def after(block, *earlier):
    return pl.pallas_call(
        nothing,
        out_shape=jax.ShapeDtypeStruct(block.shape, block.dtype),
        in_specs=[pl.BlockSpec(memory_space=pl.ANY)] * (1 + len(earlier)),
        out_specs=pl.BlockSpec(memory_space=pl.ANY),
        input_output_aliases={0: 0},
        cost_estimate=pl.CostEstimate(flops=0, bytes_accessed=0, transcendentals=0),
    )(block, *earlier)


def up_kernel(order, rows, weight, keep, send):
    del order
    part = jnp.dot(rows[...], weight[...], preferred_element_type=jnp.float32)
    half = part.shape[0] // 2
    keep[...] = part[:half].reshape(keep.shape)
    send[...] = part[half:].reshape(send.shape).astype(send.dtype)


def up_parts(order, rows, weight, halves, count, blocks):
    depth, width = weight.shape
    span = width // blocks
    tile = column_tile(span)
    tiles = span // tile
    shape = (halves, blocks, count, span)
    place = pl.BlockSpec((halves, None, count, tile), lambda b, n, order: (0, b, 0, n))
    return pl.pallas_call(
        up_kernel,
        grid_spec=pltpu.PrefetchScalarGridSpec(
            num_scalar_prefetch=1,
            grid=(blocks, tiles),
            in_specs=[
                pl.BlockSpec(rows.shape, lambda b, n, order: (0, 0)),
                pl.BlockSpec((depth, tile), lambda b, n, order: (0, order[b] * tiles + n)),
            ],
            out_specs=[place, place],
        ),
        out_shape=[
            jax.ShapeDtypeStruct(shape, jnp.float32),
            jax.ShapeDtypeStruct(shape, jnp.bfloat16),
        ],
        compiler_params=pltpu.CompilerParams(vmem_limit_bytes=VMEM_BYTES),
        cost_estimate=pl.CostEstimate(
            flops=2 * rows.shape[0] * depth * width,
            bytes_accessed=2 * depth * width + 6 * halves * count * width,
            transcendentals=0,
        ),
    )(order, rows, weight)


def block_kernel(order, rows, weight, out):
    del order
    part = jnp.dot(rows[...], weight[...], preferred_element_type=jnp.float32)
    out[...] = part.astype(out.dtype)


def up_blocks(order, rows, weight, blocks, kind):
    depth, width = weight.shape
    span = width // blocks
    tile = column_tile(span)
    tiles = span // tile
    chosen, count = order.shape[0], rows.shape[0]
    return pl.pallas_call(
        block_kernel,
        grid_spec=pltpu.PrefetchScalarGridSpec(
            num_scalar_prefetch=1,
            grid=(chosen, tiles),
            in_specs=[
                pl.BlockSpec(rows.shape, lambda b, n, order: (0, 0)),
                pl.BlockSpec((depth, tile), lambda b, n, order: (0, order[b] * tiles + n)),
            ],
            out_specs=pl.BlockSpec((None, count, tile), lambda b, n, order: (b, 0, n)),
        ),
        out_shape=jax.ShapeDtypeStruct((chosen, count, span), kind),
        compiler_params=pltpu.CompilerParams(vmem_limit_bytes=VMEM_BYTES),
        cost_estimate=pl.CostEstimate(
            flops=2 * count * depth * span * chosen,
            bytes_accessed=2 * chosen * span * (depth + 2 * count),
            transcendentals=0,
        ),
    )(order, rows, weight)


def down_kernel(order, rows, weight, keep, send, total):
    del order
    step = pl.program_id(1)
    part = transposed(rows[...], weight[...])

    @pl.when(step == 0)
    def _():
        total[...] = part

    @pl.when(step > 0)
    def _():
        total[...] += part

    @pl.when(step == pl.num_programs(1) - 1)
    def _():
        half = total.shape[0] // 2
        keep[...] = total[:half].reshape(keep.shape)
        send[...] = total[half:].reshape(send.shape).astype(send.dtype)


def down_parts(order, rows, weight, parts):
    blocks, tokens, span = rows.shape
    width = weight.shape[0]
    tile = next(t for t in (512, 384, 256, 128) if width % t == 0)
    shape = (parts // 2, tokens // parts, width)
    place = pl.BlockSpec(shape[:2] + (tile,), lambda n, b, order: (0, 0, n))
    return pl.pallas_call(
        down_kernel,
        grid_spec=pltpu.PrefetchScalarGridSpec(
            num_scalar_prefetch=1,
            grid=(width // tile, blocks),
            in_specs=[
                pl.BlockSpec((None, tokens, span), lambda n, b, order: (b, 0, 0)),
                pl.BlockSpec((tile, span), lambda n, b, order: (n, order[b])),
            ],
            out_specs=[place, place],
            scratch_shapes=[pltpu.VMEM((tokens, tile), jnp.float32)],
        ),
        out_shape=[
            jax.ShapeDtypeStruct(shape, jnp.float32),
            jax.ShapeDtypeStruct(shape, jnp.bfloat16),
        ],
        compiler_params=pltpu.CompilerParams(vmem_limit_bytes=VMEM_BYTES),
        cost_estimate=pl.CostEstimate(
            flops=2 * tokens * width * blocks * span,
            bytes_accessed=2 * blocks * span * (width + 3 * tokens) + 3 * tokens * width,
            transcendentals=0,
        ),
    )(order, rows, weight)


def active_kernel(keep, got, active):
    pre = keep[...] + got[...].astype(jnp.float32)
    active[...] = gelu_value(pre).astype(active.dtype)


def slope_kernel(keep, got, grad_keep, grad_got, grad):
    pre = keep[...] + got[...].astype(jnp.float32)
    above = grad_keep[...] + grad_got[...].astype(jnp.float32)
    grad[...] = (above * gelu_slope(pre)).astype(grad.dtype)


def on_chunk(kernel, arrays, place):
    count, span = arrays[0].shape
    tile = column_tile(span)
    here = pl.BlockSpec((count, tile), lambda n: (0, n))
    there = pl.BlockSpec((count, tile), lambda n: (place, n))
    return pl.pallas_call(
        kernel,
        grid=(span // tile,),
        in_specs=[here, here] + [there] * (len(arrays) - 2),
        out_specs=here,
        out_shape=jax.ShapeDtypeStruct((count, span), jnp.bfloat16),
        compiler_params=pltpu.CompilerParams(vmem_limit_bytes=VMEM_BYTES),
        cost_estimate=pl.CostEstimate(
            flops=20 * count * span,
            bytes_accessed=8 * count * span,
            transcendentals=count * span,
        ),
    )(*arrays)


def input_kernel(order, weight, *refs):
    del order
    pieces, out, total, stack = refs[:-3], refs[-3], refs[-2], refs[-1]
    first = (pl.program_id(0) == 0) & (pl.program_id(1) == 0)
    last = (pl.program_id(0) == pl.num_programs(0) - 1) & (
        pl.program_id(1) == pl.num_programs(1) - 1
    )

    @pl.when(first)
    def _():
        total[...] = jnp.zeros_like(total)

    row = 0
    for piece in pieces:
        for part in range(piece.shape[0]):
            stack[pl.ds(row, piece.shape[1]), :] = piece[part]
            row += piece.shape[1]
    total[...] += transposed(stack[...], weight[...])

    @pl.when(last)
    def _():
        out[...] = total[...].astype(out.dtype)


def input_parts(order, pieces, weight, blocks):
    depth, width = weight.shape
    span = width // blocks
    tile = column_tile(span)
    tiles = span // tile
    rows = sum(piece.shape[0] * piece.shape[2] for piece in pieces)
    return pl.pallas_call(
        input_kernel,
        grid_spec=pltpu.PrefetchScalarGridSpec(
            num_scalar_prefetch=1,
            grid=(blocks, tiles),
            in_specs=[
                pl.BlockSpec((depth, tile), lambda b, n, order: (0, order[b] * tiles + n))
            ]
            + [
                pl.BlockSpec(
                    (piece.shape[0], None, piece.shape[2], tile), lambda b, n, order: (0, b, 0, n)
                )
                for piece in pieces
            ],
            out_specs=pl.BlockSpec((rows, depth), lambda b, n, order: (0, 0)),
            scratch_shapes=[
                pltpu.VMEM((rows, depth), jnp.float32),
                pltpu.VMEM((rows, tile), jnp.bfloat16),
            ],
        ),
        out_shape=jax.ShapeDtypeStruct((rows, depth), jnp.bfloat16),
        compiler_params=pltpu.CompilerParams(vmem_limit_bytes=VMEM_BYTES),
        cost_estimate=pl.CostEstimate(
            flops=2 * rows * depth * width,
            bytes_accessed=2 * depth * width + 2 * rows * (depth + width),
            transcendentals=0,
        ),
    )(order, weight, *pieces)


def weight_kernel(order, columns, *refs):
    del order
    pieces, out, stack = refs[:-2], refs[-2], refs[-1]
    row = 0
    for piece in pieces:
        for part in range(piece.shape[0]):
            stack[pl.ds(row, piece.shape[1]), :] = piece[part]
            row += piece.shape[1]
    out[...] = jnp.dot(
        columns[...], stack[...], preferred_element_type=jnp.float32
    ).astype(out.dtype)


def weight_parts(order, columns, pieces, blocks):
    depth, rows = columns.shape
    span = pieces[0].shape[3]
    tile = column_tile(span)
    tiles = span // tile
    width = span * blocks
    return pl.pallas_call(
        weight_kernel,
        grid_spec=pltpu.PrefetchScalarGridSpec(
            num_scalar_prefetch=1,
            grid=(blocks, tiles),
            in_specs=[pl.BlockSpec((depth, rows), lambda b, n, order: (0, 0))]
            + [
                pl.BlockSpec(
                    (piece.shape[0], None, piece.shape[2], tile), lambda b, n, order: (0, b, 0, n)
                )
                for piece in pieces
            ],
            out_specs=pl.BlockSpec(
                (depth, tile), lambda b, n, order: (0, order[b] * tiles + n)
            ),
            scratch_shapes=[pltpu.VMEM((rows, tile), jnp.bfloat16)],
        ),
        out_shape=jax.ShapeDtypeStruct((depth, width), jnp.bfloat16),
        compiler_params=pltpu.CompilerParams(vmem_limit_bytes=VMEM_BYTES),
        cost_estimate=pl.CostEstimate(
            flops=2 * rows * depth * width,
            bytes_accessed=2 * rows * (depth + width) + 2 * depth * width,
            transcendentals=0,
        ),
    )(order, columns, *pieces)


def relative(parts, own):
    return jnp.stack(
        [
            lax.dynamic_index_in_dim(parts, own ^ s, 0, keepdims=False)
            for s in range(parts.shape[0])
        ]
    )


def halved(keep, send, axis, size, bit, down):
    while True:
        got = flip(send, axis, size, bit)
        if keep.shape[0] == 1:
            return keep[0], got[0]
        total = keep + got.astype(jnp.float32)
        half = total.shape[0] // 2
        keep, send = total[:half], total[half:].astype(jnp.bfloat16)
        bit = bit // 2 if down else bit * 2


def doubled(block, axis, size, up=False):
    bits = [1 << b for b in range(size.bit_length() - 1)]
    for bit in bits if up else bits[::-1]:
        block = jnp.concatenate([block, flip(block, axis, size, bit)], axis=0)
    return block


def natural(parts):
    return jnp.stack([parts[s] for s in reversed_bits(parts.shape[0])])


def local(ni, nj, nk, features, in_weight, out_weight, cotangent):
    tokens = features.shape[0] * ni
    depth = in_weight.shape[0]
    share = tokens // nk
    chunks = next(c for c in (4, 2, 1) if share % (16 * c) == 0)
    count = share // chunks
    own_i = lax.axis_index("ia")
    own_j = lax.axis_index("ja")
    own_k = lax.axis_index("ka")
    order = own_i ^ jnp.array(reversed_bits(ni), jnp.int32)
    swap = [(a * nj + b, b * ni + a) for a in range(ni) for b in range(nj)]
    crosswise = [chunk == 1 for chunk in range(chunks)]

    if ni == nj:
        turned = lax.ppermute(features, ("ia", "ja"), swap)
        feature_cols = lax.all_gather(turned, "ja", axis=0, tiled=True)
    else:
        feature_rows = lax.all_gather(features, "ja", axis=1, tiled=True)
        feature_cols = lax.all_to_all(
            feature_rows, "ia", split_axis=1, concat_axis=0, tiled=True
        )
    shuffled = relative(feature_cols.reshape(nk, share, depth), own_k)
    shuffled = shuffled.reshape(nk, chunks, count, depth).transpose(1, 0, 2, 3)
    shuffled = shuffled.reshape(tokens, depth)

    half = ni // 2
    straight = [chunk for chunk in range(chunks) if not crosswise[chunk]]
    across = [chunk for chunk in range(chunks) if crosswise[chunk]]
    rows_of = [shuffled[c * nk * count : (c + 1) * nk * count] for c in range(chunks)]
    kept = {}
    arrived = []

    def product(place):
        rows = rows_of[straight[place]]
        if place == 1:
            rows = after(rows, kept[straight[0]][1])
        if place > 1:
            rows = after(rows, arrived[place - 2])
        kept[straight[place]] = up_parts(order, rows, in_weight, nk // 2, count, ni)

    product(0)
    if len(straight) > 1:
        product(1)
    begun = kept[straight[:2][-1]][1]
    crossing = {}
    for chunk in across:
        rows = after(rows_of[chunk], begun)
        send = up_blocks(order[half:], rows, in_weight, ni, jnp.bfloat16)
        keep = up_blocks(order[:half], rows, in_weight, ni, jnp.float32)
        crossing[chunk] = halved(keep, send, "ia", ni, 1, False)

    if ni == nj:
        cotangent = after(cotangent, turned)
    cot_tokens = relative(natural(doubled(cotangent[None], "ia", ni)), own_i)
    cot_tokens = relative(cot_tokens.reshape(nk, share, -1), own_k)
    cot_tokens = after(cot_tokens.reshape(1, tokens, -1), begun)
    cot_parts = doubled(cot_tokens, "ja", nj)
    cot_order = own_j ^ jnp.array(reversed_bits(nj), jnp.int32)
    if cot_parts.shape[-1] % 128:
        cot_parts = relative(natural(cot_parts), own_j).transpose(1, 0, 2)
        cot_parts = cot_parts.reshape(1, tokens, -1)
        cot_order = jnp.zeros((1,), jnp.int32)
    grad_keep, grad_send = down_parts(cot_order, cot_parts, out_weight, nk)

    sums = [None] * chunks
    for place, chunk in enumerate(straight):
        if place > 1:
            product(place)
        keep, send = kept[chunk]
        if place:
            send = after(send, arrived[-1])
        keep, came = halved(keep, send, "ka", nk, nk // 2, True)
        arrived.append(came)
        total = keep + came.astype(jnp.float32)
        sums[chunk] = halved(
            total[:half], total[half:].astype(jnp.bfloat16), "ia", ni, 1, False
        )
    came = arrived[-1]
    for chunk, later in zip(straight, arrived[1:]):
        keep, got = sums[chunk]
        sums[chunk] = keep, after(got, later)
    for chunk in across:
        keep, got = crossing[chunk]
        got = after(got, arrived[-2:][0])
        total = (keep + got.astype(jnp.float32)).reshape(nk, count, -1)
        send = after(total[nk // 2 :].astype(jnp.bfloat16), came, grad_send)
        sums[chunk] = halved(total[: nk // 2], send, "ka", nk, nk // 2, True)
        came = sums[chunk][1]
    grad_keep, grad_got = halved(
        grad_keep, after(grad_send, came), "ka", nk, nk // 2, True
    )
    actives = [on_chunk(active_kernel, sums[chunk], 0) for chunk in range(chunks)]
    own_active = jnp.concatenate(actives, axis=0)
    parts = after(own_active, grad_got)[None]
    active_parts = doubled(parts, "ka", nk, True)
    active_rows = active_parts.reshape(tokens, -1)
    came = active_parts

    slopes = {}
    slope = own_active
    for chunk in range(chunks):
        arrays = list(sums[chunk]) + [grad_keep, grad_got]
        arrays[1] = after(arrays[1], slope)
        slope = on_chunk(slope_kernel, arrays, chunk)
        slopes[chunk] = slope[None]
    gathered = [
        lax.all_gather(slopes[chunk], "ia", axis=0, tiled=True) for chunk in range(chunks)
    ]
    plain = jnp.arange(ni, dtype=jnp.int32)

    def output_over_ja(*gates):
        active_tokens = relative(active_parts, own_k).reshape(ni, tokens // ni, -1)
        active_tokens = natural(relative(active_tokens, own_i)).reshape(tokens, -1)
        active_tokens = after(active_tokens, *gates)
        if out_weight.shape[1] // nj % 128:
            output_part = jnp.dot(
                active_tokens, out_weight, preferred_element_type=jnp.float32
            )
            output_sum = lax.psum_scatter(
                output_part.astype(jnp.bfloat16), "ja", scatter_dimension=1, tiled=True
            ).astype(jnp.float32)
        else:
            send = up_blocks(
                cot_order[nj // 2 :], active_tokens, out_weight, nj, jnp.bfloat16
            )
            keep = up_blocks(
                cot_order[: nj // 2], active_tokens, out_weight, nj, jnp.float32
            )
            keep, got = halved(keep, send, "ja", nj, 1, False)
            output_sum = keep + got.astype(jnp.float32)
        return output_sum

    pieces_of = []
    input_rows = []
    for chunk in range(chunks):
        ready = slopes[chunks - 1] if chunk == 0 else came
        block = after(gathered[chunk][None], came, ready, *input_rows[-2:-1])
        pieces = [block]
        bit = 1
        while bit < nk:
            came = flip(block, "ka", nk, bit)
            pieces.append(came)
            bit *= 2
            if bit < nk:
                block = jnp.concatenate([block, came], axis=0)
        arrived.append(came)
        pieces_of.append(pieces)
        if chunk == 0:
            output_sum = output_over_ja(came, gathered[: chunks // 2][-1])
        if chunk == chunks - 1:
            out_weight_grad = weight_parts(
                cot_order,
                after(active_rows.T, arrived[-2]),
                [cot_parts[None]],
                cot_parts.shape[0],
            )
            earlier = [output_sum, out_weight_grad] + input_rows
            pieces = [after(pieces[0], *earlier)] + pieces[1:]
        input_rows.append(input_parts(plain, pieces, in_weight, ni))
    last_rows = input_rows[-1]
    input_rows = [rows.reshape(nk, count, depth) for rows in input_rows]
    in_weight_grad = weight_parts(
        plain,
        after(shuffled.T, last_rows),
        [piece for pieces in pieces_of for piece in pieces],
        ni,
    )

    input_part = jnp.stack(input_rows, axis=1).reshape(nk, share, depth)
    input_part = relative(input_part, own_k).reshape(tokens, depth)
    if ni == nj:
        parts = natural(relative(input_part.reshape(nj, tokens // nj, depth), own_j))
        keep, got = halved(parts[: nj // 2], parts[nj // 2 :], "ja", nj, 1, False)
        input_sum = (keep + got.astype(jnp.float32)).astype(jnp.bfloat16)
        feature_grad = lax.ppermute(input_sum, ("ia", "ja"), swap)
    else:
        input_full = lax.all_to_all(
            input_part, "ia", split_axis=0, concat_axis=1, tiled=True
        )
        feature_grad = lax.psum_scatter(
            input_full, "ja", scatter_dimension=1, tiled=True
        )

    output_sum = output_sum.reshape(ni, tokens // ni, -1)
    send = output_sum[half:].astype(jnp.bfloat16)
    keep, got = halved(output_sum[:half], send, "ia", ni, 1, False)
    layer_out = (keep + got.astype(jnp.float32)).astype(jnp.bfloat16)
    return (layer_out, feature_grad, in_weight_grad, out_weight_grad)


def solution(mesh):
    placed = (
        P("ia", ("ka", "ja")),
        P(("ka", "ia"), "ja"),
        P(("ja", "ia"), "ka"),
        P("ia", ("ka", "ja")),
    )
    return jax.shard_map(
        functools.partial(local, *(mesh.shape[axis] for axis in ("ia", "ja", "ka"))),
        mesh=mesh,
        in_specs=placed,
        out_specs=(
            P("ia", ("ka", "ja")),
            P("ia", ("ka", "ja")),
            P(("ka", "ia"), "ja"),
            P(("ja", "ia"), "ka"),
        ),
        check_vma=False,
    )
```
